32 devices in a mesh: rep: 4 (over x, core), shard: 8 (over z, y).
Axes of the slice: x: 2, y: 2, z: 4, core: 2. Of those that a mesh axis runs over, the one named last changes fastest.
Arguments:
- tokens_in: bfloat16 [16384, 8192], P(('rep', 'shard'))
- key_cotangent: bfloat16 [16384, 1024], P(('rep', 'shard'))
- token_counts: int32 [4, 32], P(None, ('rep', 'shard')), may hold values from 128 to 512, as said below
- grad_accum: float32 [8192, 1024], P('shard')
- key_weight: float32 [8192, 1024], P('shard')
- row_moment: float32 [8192], P('shard'), may hold values from 0.1 to 0.3
- col_moment: float32 [1024], replicated, may hold values from 0.0001 to 0.001
Outputs:
- new_weight: float32 [8192, 1024], P('shard')
- direction: float32 [8192, 1024], P('shard')
- new_row: float32 [8192], P('shard')
- new_col: float32 [1024], replicated
The draws below stay inside these ranges and needn't reach their ends.
Inputs may be any that keep to these rules, and one draw needn't show every extreme that they name: Column d of token_counts belongs to device d in the order rep, then shard; the live tokens of the last microbatch are the first token_counts[3, d] of that device's 512 slots. Some entry equals 512 and some equals 128.
All inputs are finite; a program needn't handle non-finite values.
Results may differ from the reference program's by a relative error of at most 0.0003.
Values may be sent and summed in bfloat16 or wider, within the bound.
A program may use at most 128 MiB of HBM per device.

```python
import math
import jax
import jax.numpy as jnp
from jax import lax

D = 8192
KV = 1024
TOK_DEV = 512
MICRO = 4
TOKENS = 16384
N_REP = 4
N_SHARD = 8


def spread_scales(key, count, low, high):
    unit = jax.random.uniform(key, (count,), jnp.float32)
    return jnp.exp(jnp.log(low) + unit * (jnp.log(high) - jnp.log(low)))


def row_rise():
    index = jnp.arange(D, dtype=jnp.int32)
    block = D // N_SHARD
    within = (index % block).astype(jnp.float32) / block
    across = (index // block).astype(jnp.float32) / N_SHARD
    return jnp.exp(jnp.log(3.0) * within + jnp.log(3.0) * across)


def feature_scales(key):
    return spread_scales(jax.random.fold_in(key, 101), D, 0.7, 1.4) * row_rise()


def column_scales(key):
    return spread_scales(jax.random.fold_in(key, 202), KV, 0.3, 3.0)


def draw_tokens_in(key, part):
    inner = jax.random.fold_in(key, 1)
    base = jax.random.normal(inner, (TOKENS, D), jnp.float32)
    return (base * feature_scales(key)[None, :]).astype(jnp.bfloat16)


def draw_key_cotangent(key, part):
    inner = jax.random.fold_in(key, 2)
    base = jax.random.normal(inner, (TOKENS, KV), jnp.float32)
    factor = 0.0125 * jnp.sqrt(1.0 * N_REP * N_SHARD * TOK_DEV)
    return (base * column_scales(key)[None, :] * factor).astype(jnp.bfloat16)


def draw_grad_accum(key, part):
    inner = jax.random.fold_in(key, 4)
    base = jax.random.normal(inner, (D, KV), jnp.float32)
    factor = 0.025 * N_REP * N_SHARD * TOK_DEV
    return base * feature_scales(key)[:, None] * column_scales(key)[None, :] * factor


def draw_key_weight(key, part):
    inner = jax.random.fold_in(key, 9)
    base = jax.random.normal(inner, (D, KV), jnp.float32)
    scales = spread_scales(jax.random.fold_in(key, 10), D, 0.7, 1.4) * row_rise() * 0.3
    return base * scales[:, None]


def draw_token_counts(key, part):
    entries = MICRO * N_REP * N_SHARD
    counts = jax.random.randint(jax.random.fold_in(key, 5), (entries,), TOK_DEV // 4, TOK_DEV + 1, jnp.int32)
    order = jax.random.permutation(jax.random.fold_in(key, 6), entries)
    counts = counts.at[order[0]].set(TOK_DEV).at[order[1]].set(TOK_DEV // 4)
    return counts.reshape(MICRO, N_REP * N_SHARD)


def steps_of(stream_key, dims, cuts, least, largest):
    gain, own = 1.0, jax.random.fold_in(stream_key, 6)
    for position, blocks in cuts:
        steps = jnp.exp(jax.random.uniform(jax.random.fold_in(own, position), (blocks,), jnp.float32, least / len(cuts), largest / len(cuts)))
        gain = gain * jnp.repeat(steps, dims[position] // blocks).reshape([-1 if axis == position else 1 for axis in range(len(dims))])
    return gain


def setup_inputs(seed: int = 0) -> dict:
    seeds = jax.random.split(jax.random.key(seed), 8)
    tokens_in = draw_tokens_in(jax.random.fold_in(seeds[7], 71), 0)
    key_cotangent = draw_key_cotangent(jax.random.fold_in(seeds[7], 71), 0)
    token_counts = draw_token_counts(jax.random.fold_in(seeds[7], 71), 0)
    grad_accum = draw_grad_accum(jax.random.fold_in(seeds[7], 71), 0)
    key_weight = draw_key_weight(jax.random.fold_in(seeds[7], 71), 0)
    row_moment = jnp.clip(jnp.exp(math.log(0.3) - 1.0986123 * jax.random.uniform(seeds[5], (D,), jnp.float32) ** steps_of(seeds[5], (D,), ((0, 8),), -0.2, 0.2)), 0.1, 0.3)
    col_moment = jnp.clip(jnp.exp(jax.random.uniform(seeds[6], (KV,), jnp.float32, math.log(0.0001), math.log(0.001))), 0.0001, 0.001)
    return dict(tokens_in=tokens_in, key_cotangent=key_cotangent, token_counts=token_counts, grad_accum=grad_accum, key_weight=key_weight, row_moment=row_moment, col_moment=col_moment)


eps_square = 1e-30
decay_rate = 0.6
clip_bound = 1.0
step_rate = 0.05

def reference(tokens_in, key_cotangent, token_counts, grad_accum, key_weight, row_moment, col_moment):
    total = jnp.sum(token_counts).astype(jnp.float32)
    live = token_counts[MICRO - 1]
    slots = jnp.arange(TOKENS, dtype=jnp.int32)
    owner = (slots // TOK_DEV).astype(jnp.int32)
    keep = slots % TOK_DEV < live[owner]
    masked = jnp.where(keep[:, None], key_cotangent, jnp.zeros((), key_cotangent.dtype))
    last_grad = lax.dot_general(tokens_in, masked, (((0,), (0,)), ((), ())), preferred_element_type=jnp.float32)
    grad = (grad_accum + last_grad) / total
    squares = grad * grad + eps_square
    new_row = decay_rate * row_moment + (1.0 - decay_rate) * lax.optimization_barrier(jnp.mean(squares, axis=1))
    new_col = decay_rate * col_moment + (1.0 - decay_rate) * lax.optimization_barrier(jnp.mean(squares, axis=0))
    update = grad * lax.rsqrt(new_row[:, None] * new_col[None, :])
    clip = jnp.maximum(1.0, jnp.sqrt(jnp.mean(update * update)) / clip_bound)
    direction = update / clip
    weight_rms = jnp.sqrt(jnp.mean(key_weight * key_weight))
    new_weight = key_weight - step_rate * weight_rms * direction
    return (new_weight, direction, new_row, new_col)
```

```python
import functools

import jax
import jax.numpy as jnp
from jax import lax
from jax.experimental import pallas as pl
from jax.experimental.pallas import tpu as pltpu
from jax.sharding import PartitionSpec as P

EPS = 1e-30
DECAY = 0.6
CLIP = 1.0
RATE = 0.05
MESH = pl.DeviceIdType.MESH
WINDOW = 3
F32 = jnp.float32


def lo_size(shard):
    return 2 if shard == 8 else 4


def kernel(dims, t_ref, k_ref, cnt_ref, acc_ref, w_ref, row_ref, g_out, s_out,
           t_buf, k_buf, part, y_buf, z_buf, acc_v, w_v, row_v, g_buf,
           c1, c2, c3, s1, s2, s3,
           t_local, t_send, t_recv, k_local, kx_send, kx_recv, kc_send, kc_recv,
           kf_send, kf_recv, y_send, y_recv, z_send, z_recv, in_sem,
           g_local, gx_send, gx_recv, gc_send, gc_recv, gf_send, gf_recv,
           a_send, a_recv, b_send, b_recv):
    R, S, H, L, G, sub, tok, natural = dims
    X = R // 2
    NG = L // G
    NCH = H * NG
    width = G * sub
    D = S * R * sub
    rep, shard = lax.axis_index("rep"), lax.axis_index("shard")
    x, c = rep // 2, rep % 2
    sib = x * 2 + (1 - c)
    hi, lo = shard // L, shard % L
    g0 = lo // G

    def dev_rep(r):
        return (r, shard)

    def dev_lo(l):
        return (rep, hi * L + l)

    def dev_hi(h):
        return (rep, h * L + lo)

    def rcopy(src, dst, ss, rs, dev):
        return pltpu.make_async_remote_copy(src_ref=src, dst_ref=dst, send_sem=ss, recv_sem=rs,
                                            device_id=dev, device_id_type=MESH)

    barrier = pltpu.get_barrier_semaphore()
    peers = ([dev_rep((rep + p) % R) for p in range(1, R)] + [dev_lo((lo + p) % L) for p in range(1, L)]
             + [dev_hi((hi + p) % H) for p in range(1, H)])
    for dev in peers:
        pl.semaphore_signal(barrier, inc=1, device_id=dev, device_id_type=MESH)
    in_copies = []
    rows = pl.ds(pl.multiple_of(rep * sub, sub), sub)
    for i, (src, dst) in enumerate(((acc_ref, acc_v), (w_ref, w_v), (row_ref, row_v))):
        cp = pltpu.make_async_copy(src.at[rows], dst, in_sem.at[i])
        cp.start()
        in_copies.append(cp)
    my_tok = pl.ds(pl.multiple_of(rep * tok, tok), tok)
    k_cp = pltpu.make_async_copy(k_ref, k_buf.at[my_tok], k_local.at[0])
    k_cp.start()
    pl.semaphore_wait(barrier, len(peers))

    def reduce_all(first, b1, b2, b3, sends, recvs):
        value = first
        base = 0
        for buf, n, me, dev in ((b1, R, rep, dev_rep), (b2, L, lo, dev_lo), (b3, H, hi, dev_hi)):
            buf[me] = value
            cps = []
            for p in range(1, n):
                cp = rcopy(buf.at[me], buf.at[me], sends.at[base + p - 1], recvs.at[base + p - 1], dev((me + p) % n))
                cp.start()
                cps.append(cp)
            for cp in cps:
                cp.wait_send()
                cp.wait_recv()
            base += n - 1
            value = buf[0]
            for i in range(1, n):
                value = value + buf[i]
        return value

    k_sib = rcopy(k_ref, k_buf.at[my_tok], kc_send.at[0], kc_recv.at[0], dev_rep(sib))
    k_far = [rcopy(k_ref, k_buf.at[my_tok], kx_send.at[q - 1], kx_recv.at[q - 1],
                   dev_rep(((x + q) % X) * 2 + c)) for q in range(1, X)]
    for cp in k_far:
        cp.start()
    k_sib.start()

    def k_fwd(q):
        src = ((x + X - q) % X) * 2 + c
        at = pl.ds(pl.multiple_of(src * tok, tok), tok)
        return rcopy(k_buf.at[at], k_buf.at[at], kf_send.at[q - 1], kf_recv.at[q - 1], dev_rep(sib))

    def block_of(t):
        return ((hi + 1 + t // NG) % H) * L + ((g0 + 1 + t % NG) % NG) * G

    def t_cols(r, s0):
        if natural:
            off = s0 * (R * sub) + r * sub
        else:
            off = r * (S * sub) + s0 * sub
        return pl.ds(pl.multiple_of(off, width), width)

    def t_dst(s0):
        return t_buf.at[my_tok, pl.ds(pl.multiple_of(s0 * sub, width), width)]

    def t_loc(t):
        s0 = block_of(t)
        return pltpu.make_async_copy(t_ref.at[:, t_cols(rep, s0)], t_dst(s0), t_local.at[t])

    def t_rem(t, p):
        s0 = block_of(t)
        to = (rep + p) % R
        return rcopy(t_ref.at[:, t_cols(to, s0)], t_dst(s0), t_send.at[p - 1, t], t_recv.at[p - 1, t], dev_rep(to))

    def t_start(t):
        for p in range(1, R):
            t_rem(t, p).start()
        t_loc(t).start()

    for t in range(min(WINDOW, NCH)):
        t_start(t)

    total = reduce_all(cnt_ref[...], c1, c2, c3, a_send, a_recv)

    for q in range(1, X):
        k_far[q - 1].wait_recv()
        k_fwd(q).start()
    k_cp.wait()
    k_sib.wait_recv()
    for q in range(1, X):
        k_fwd(q).wait_recv()

    def part_rows(s, n=1):
        return pl.ds(pl.multiple_of(s * sub, n * sub), n * sub)

    def y_copy(k, lt, p):
        s = ((hi + 1 + k) % H) * L + lt
        return rcopy(part.at[part_rows(s)], y_buf.at[p - 1, k], y_send.at[p - 1, k], y_recv.at[p - 1, k], dev_lo(lt))

    def z_copy(k):
        h = (hi + 1 + k) % H
        return rcopy(part.at[part_rows(h * L + lo)], z_buf.at[k], z_send.at[k], z_recv.at[k], dev_hi(h))

    def y_add(k):
        s = ((hi + 1 + k) % H) * L + lo
        at = part_rows(s)
        for p in range(1, L):
            y_copy(k, (lo + p) % L, p).wait_recv()
        value = part[at, :]
        for p in range(1, L):
            value = value + y_buf[p - 1, k]
        part[at, :] = value

    def step(k, carry):
        for j in range(NG):
            t = k * NG + j
            t_loc(t).wait()
            for p in range(1, R):
                t_rem(t, p).wait_recv()

            @pl.when(t + WINDOW < NCH)
            def _():
                t_start(t + WINDOW)

            s0 = block_of(t)
            at = pl.ds(pl.multiple_of(s0 * sub, width), width)
            part[at, :] = lax.dot_general(t_buf[:, at], k_buf[...], (((0,), (0,)), ((), ())),
                                          preferred_element_type=F32)
            for i in range(G):
                lt = s0 % L + i
                p = (lt - lo + L) % L
                if G == 1:
                    if j < NG - 1:
                        y_copy(k, lt, p).start()
                else:
                    @pl.when(p > 0)
                    def _():
                        y_copy(k, lt, p).start()
            if j == 0:
                @pl.when(k > 0)
                def _():
                    y_add(k - 1)
                    z_copy(k - 1).start()
        return carry

    lax.fori_loop(0, H, step, 0)
    y_add(H - 1)
    for k in range(H - 1):
        z_copy(k).wait_recv()
    for cp in in_copies:
        cp.wait()
    value = part[part_rows(shard), :]
    for k in range(H - 1):
        value = value + z_buf[k]
    grad = (acc_v[...] + value) / total[0:1, 0:1]
    g_buf[:, :acc_v.shape[1]] = grad
    g2 = grad * grad
    squares = g2 + EPS
    mean = jnp.sum(squares, axis=1, keepdims=True) / squares.shape[1]
    new_row = DECAY * row_v[...] + (1.0 - DECAY) * mean
    g_buf[:, acc_v.shape[1]:] = new_row

    g_cp = pltpu.make_async_copy(g_buf, g_out.at[rows], g_local.at[0])
    g_sib = rcopy(g_buf, g_out.at[rows], gc_send.at[0], gc_recv.at[0], dev_rep(sib))
    g_far = [rcopy(g_buf, g_out.at[rows], gx_send.at[q - 1], gx_recv.at[q - 1],
                   dev_rep(((x + q) % X) * 2 + c)) for q in range(1, X)]
    for cp in g_far:
        cp.start()
    g_sib.start()
    g_cp.start()

    col = jnp.sum(squares, axis=0, keepdims=True)
    upd = jnp.sum(g2 * (1.0 / new_row[:, :1]), axis=0, keepdims=True)
    w = w_v[...]
    wsq = jnp.sum(w * w, axis=0, keepdims=True)
    stats = jnp.concatenate([col, upd, wsq, jnp.zeros((5, col.shape[1]), F32)], axis=0)
    s_out[...] = reduce_all(stats, s1, s2, s3, b_send, b_recv)

    def g_fwd(q):
        src = ((x + X - q) % X) * 2 + c
        at = pl.ds(pl.multiple_of(src * sub, sub), sub)
        return rcopy(g_out.at[at], g_out.at[at], gf_send.at[q - 1], gf_recv.at[q - 1], dev_rep(sib))

    for q in range(1, X):
        g_far[q - 1].wait_recv()
        g_fwd(q).start()
    g_cp.wait()
    g_sib.wait()

    k_sib.wait_send()
    for q in range(1, X):
        k_far[q - 1].wait_send()
        k_fwd(q).wait_send()
        g_far[q - 1].wait_send()
        g_fwd(q).wait()

    def t_done(t, carry):
        for p in range(1, R):
            t_rem(t, p).wait_send()
        return carry

    lax.fori_loop(0, NCH, t_done, 0)
    for k in range(H):
        for p in range(1, L):
            y_copy(k, (lo + p) % L, p).wait_send()
        if k < H - 1:
            z_copy(k).wait_send()


def body(R, S, L, tokens_in, key_cotangent, token_counts, grad_accum, key_weight, row_moment, col_moment):
    tok, D = tokens_in.shape
    KV = key_cotangent.shape[1]
    H = S // L
    sub = D // (R * S)
    B = R * sub
    X = R // 2
    natural = sub % 128 == 0
    G = 1 if natural else 128 // sub
    NCH = S // G
    live = token_counts[token_counts.shape[0] - 1, 0]
    keep = lax.broadcasted_iota(jnp.int32, (tok, 1), 0) < live
    masked = jnp.where(keep, key_cotangent, jnp.zeros((), key_cotangent.dtype))
    count = jnp.full((8, 128), jnp.sum(token_counts).astype(F32))
    rows = jnp.broadcast_to(row_moment[:, None], (B, 128))
    tokens = tokens_in
    if not natural:
        tokens = tokens.reshape(tok, S, R, sub).transpose(0, 2, 1, 3).reshape(tok, D)
    dims = (R, S, H, L, G, sub, tok, natural)
    any_spec = pl.BlockSpec(memory_space=pl.ANY)
    vmem = pl.BlockSpec(memory_space=pltpu.VMEM)
    dma = pltpu.SemaphoreType.DMA
    n_all = (R - 1) + (L - 1) + (H - 1)
    X1 = max(X - 1, 1)
    grads, stats = pl.pallas_call(
        functools.partial(kernel, dims),
        out_shape=(jax.ShapeDtypeStruct((B, KV + 128), F32), jax.ShapeDtypeStruct((8, KV), F32)),
        in_specs=[any_spec, any_spec, vmem, any_spec, any_spec, any_spec],
        out_specs=(any_spec, vmem),
        scratch_shapes=[
            pltpu.VMEM((R * tok, S * sub), jnp.bfloat16),
            pltpu.VMEM((R * tok, KV), jnp.bfloat16),
            pltpu.VMEM((S * sub, KV), F32),
            pltpu.VMEM((L - 1, H, sub, KV), F32),
            pltpu.VMEM((H - 1, sub, KV), F32),
            pltpu.VMEM((sub, KV), F32),
            pltpu.VMEM((sub, KV), F32),
            pltpu.VMEM((sub, 128), F32),
            pltpu.VMEM((sub, KV + 128), F32),
            pltpu.VMEM((R, 8, 128), F32),
            pltpu.VMEM((L, 8, 128), F32),
            pltpu.VMEM((H, 8, 128), F32),
            pltpu.VMEM((R, 8, KV), F32),
            pltpu.VMEM((L, 8, KV), F32),
            pltpu.VMEM((H, 8, KV), F32),
            dma((NCH,)), dma((R - 1, NCH)), dma((R - 1, NCH)),
            dma((1,)), dma((X1,)), dma((X1,)), dma((1,)), dma((1,)), dma((X1,)), dma((X1,)),
            dma((L - 1, H)), dma((L - 1, H)), dma((H - 1,)), dma((H - 1,)),
            dma((3,)),
            dma((1,)), dma((X1,)), dma((X1,)), dma((1,)), dma((1,)), dma((X1,)), dma((X1,)),
            dma((n_all,)), dma((n_all,)), dma((n_all,)), dma((n_all,)),
        ],
        compiler_params=pltpu.CompilerParams(collective_id=0, has_side_effects=True,
                                             vmem_limit_bytes=50 * 1024 * 1024),
        cost_estimate=pl.CostEstimate(flops=2 * tok * D * KV, bytes_accessed=24 * 1024 * 1024, transcendentals=0),
    )(tokens, masked, count, grad_accum, key_weight, rows)
    entries = D * KV
    new_col = DECAY * col_moment + (1.0 - DECAY) * (stats[0] / D)
    update_sq = jnp.sum(stats[1] / new_col)
    weight_sum = jnp.sum(stats[2])
    new_row = grads[:, KV]
    clip = jnp.maximum(1.0, jnp.sqrt(update_sq / entries) / CLIP)
    direction = grads[:, :KV] * lax.rsqrt(new_row[:, None] * new_col[None, :]) / clip
    weight_rms = jnp.sqrt(weight_sum / entries)
    new_weight = key_weight - RATE * weight_rms * direction
    return (new_weight, direction, new_row, new_col)


def solution(mesh):
    R, S = mesh.shape["rep"], mesh.shape["shard"]
    in_specs = (
        P(("rep", "shard"), None),
        P(("rep", "shard"), None),
        P(None, ("rep", "shard")),
        P("shard", None),
        P("shard", None),
        P("shard"),
        P(),
    )
    out_specs = (P("shard", None), P("shard", None), P("shard"), P())
    return jax.shard_map(functools.partial(body, R, S, lo_size(S)), mesh=mesh, in_specs=in_specs,
                         out_specs=out_specs, check_vma=False)
```

```python
import functools

import jax
import jax.numpy as jnp
from jax import lax
from jax.experimental import pallas as pl
from jax.experimental.pallas import tpu as pltpu
from jax.sharding import PartitionSpec as P

EPS = 1e-30
DECAY = 0.6
CLIP = 1.0
RATE = 0.05
MESH = pl.DeviceIdType.MESH
EARLY = 0
WINDOW = 4
F32 = jnp.float32


def lo_size(shard):
    return 2 if shard == 8 else 4


def kernel(dims, t_ref, k_ref, cnt_ref, acc_ref, w_ref, row_ref, g_out, s_out,
           t_buf, k_buf, part, y_buf, z_buf, acc_v, w_v, row_v, g_buf,
           c1, c2, c3, s1, s2, s3,
           t_local, t_send, t_recv, k_local, kx_send, kx_recv, kc_send, kc_recv,
           kf_send, kf_recv, y_send, y_recv, z_send, z_recv, in_sem,
           g_local, gx_send, gx_recv, gc_send, gc_recv, gf_send, gf_recv,
           a_send, a_recv, b_send, b_recv):
    R, S, H, L, G, sub, tok, natural = dims
    X = R // 2
    NG = L // G
    NCH = H * NG
    width = G * sub
    D = S * R * sub
    rep, shard = lax.axis_index("rep"), lax.axis_index("shard")
    x, c = rep // 2, rep % 2
    sib = x * 2 + (1 - c)
    hi, lo = shard // L, shard % L
    g0 = lo // G

    def target(k):
        return (hi + jnp.where(k == H - 1, 0, (k + H // 2 - 1) % (H - 1) + 1)) % H

    def dev_rep(r):
        return (r, shard)

    def dev_lo(l):
        return (rep, hi * L + l)

    def dev_hi(h):
        return (rep, h * L + lo)

    def rcopy(src, dst, ss, rs, dev):
        return pltpu.make_async_remote_copy(src_ref=src, dst_ref=dst, send_sem=ss, recv_sem=rs,
                                            device_id=dev, device_id_type=MESH)

    barrier = pltpu.get_barrier_semaphore()
    peers = ([dev_rep((rep + p) % R) for p in range(1, R)] + [dev_lo((lo + p) % L) for p in range(1, L)]
             + [dev_hi((hi + p) % H) for p in range(1, H)])
    for dev in peers:
        pl.semaphore_signal(barrier, inc=1, device_id=dev, device_id_type=MESH)
    in_copies = []
    rows = pl.ds(pl.multiple_of(rep * sub, sub), sub)
    for i, (src, dst) in enumerate(((acc_ref, acc_v), (w_ref, w_v), (row_ref, row_v))):
        cp = pltpu.make_async_copy(src.at[rows], dst, in_sem.at[i])
        cp.start()
        in_copies.append(cp)
    my_tok = pl.ds(pl.multiple_of(rep * tok, tok), tok)
    k_cp = pltpu.make_async_copy(k_ref, k_buf.at[my_tok], k_local.at[0])
    k_cp.start()
    micro = cnt_ref.shape[0]
    count = cnt_ref[0, 0]
    for i in range(1, micro):
        count = count + cnt_ref[i, 0]
    k_cp.wait()
    keep = lax.broadcasted_iota(jnp.int32, (tok, 1), 0) < cnt_ref[micro - 1, 0]
    k_buf[my_tok, :] = jnp.where(keep, k_buf[my_tok, :], jnp.zeros((), k_buf.dtype))
    pl.semaphore_wait(barrier, len(peers))

    def reduce_all(first, b1, b2, b3, sends, recvs):
        value = first
        base = 0
        for buf, n, me, dev in ((b1, R, rep, dev_rep), (b2, L, lo, dev_lo), (b3, H, hi, dev_hi)):
            buf[me] = value
            cps = []
            for p in range(1, n):
                cp = rcopy(buf.at[me], buf.at[me], sends.at[base + p - 1], recvs.at[base + p - 1], dev((me + p) % n))
                cp.start()
                cps.append(cp)
            for cp in cps:
                cp.wait_send()
                cp.wait_recv()
            base += n - 1
            value = buf[0]
            for i in range(1, n):
                value = value + buf[i]
        return value

    k_sib = rcopy(k_buf.at[my_tok], k_buf.at[my_tok], kc_send.at[0], kc_recv.at[0], dev_rep(sib))
    k_far = [rcopy(k_buf.at[my_tok], k_buf.at[my_tok], kx_send.at[q - 1], kx_recv.at[q - 1],
                   dev_rep(((x + q) % X) * 2 + c)) for q in range(1, X)]
    for cp in k_far:
        cp.start()
    k_sib.start()

    def k_fwd(q):
        src = ((x + X - q) % X) * 2 + c
        at = pl.ds(pl.multiple_of(src * tok, tok), tok)
        return rcopy(k_buf.at[at], k_buf.at[at], kf_send.at[q - 1], kf_recv.at[q - 1], dev_rep(sib))

    def block_of(t):
        return target(t // NG) * L + ((g0 + 1 + t % NG) % NG) * G

    def t_cols(r, s0):
        if natural:
            off = s0 * (R * sub) + r * sub
        else:
            off = r * (S * sub) + s0 * sub
        return pl.ds(pl.multiple_of(off, width), width)

    def t_dst(s0):
        return t_buf.at[my_tok, pl.ds(pl.multiple_of(s0 * sub, width), width)]

    def t_loc(t):
        s0 = block_of(t)
        return pltpu.make_async_copy(t_ref.at[:, t_cols(rep, s0)], t_dst(s0), t_local.at[t])

    def t_rem(t, p):
        s0 = block_of(t)
        to = (rep + p) % R
        return rcopy(t_ref.at[:, t_cols(to, s0)], t_dst(s0), t_send.at[p - 1, t], t_recv.at[p - 1, t], dev_rep(to))

    def t_start(t):
        for p in range(1, R):
            t_rem(t, p).start()
        t_loc(t).start()

    for t in range(EARLY):
        t_start(t)

    total = reduce_all(jnp.full((8, 128), count.astype(F32)), c1, c2, c3, a_send, a_recv)

    for q in range(1, X):
        k_far[q - 1].wait_recv()
        k_fwd(q).start()
    for t in range(EARLY, min(WINDOW, NCH)):
        t_start(t)
    k_sib.wait_recv()
    for q in range(1, X):
        k_fwd(q).wait_recv()

    def part_rows(s, n=1):
        return pl.ds(pl.multiple_of(s * sub, n * sub), n * sub)

    def y_copy(k, lt, p):
        s = target(k) * L + lt
        return rcopy(part.at[part_rows(s)], y_buf.at[p - 1, k], y_send.at[p - 1, k], y_recv.at[p - 1, k], dev_lo(lt))

    def z_copy(k):
        h = target(k)
        return rcopy(part.at[part_rows(h * L + lo)], z_buf.at[k], z_send.at[k], z_recv.at[k], dev_hi(h))

    def y_add(k):
        s = target(k) * L + lo
        at = part_rows(s)
        for p in range(1, L):
            y_copy(k, (lo + p) % L, p).wait_recv()
        value = part[at, :]
        for p in range(1, L):
            value = value + y_buf[p - 1, k]
        part[at, :] = value

    def step(k, carry):
        for j in range(NG):
            t = k * NG + j
            t_loc(t).wait()
            for p in range(1, R):
                t_rem(t, p).wait_recv()

            @pl.when(t + WINDOW < NCH)
            def _():
                t_start(t + WINDOW)

            s0 = block_of(t)
            at = pl.ds(pl.multiple_of(s0 * sub, width), width)
            part[at, :] = lax.dot_general(t_buf[:, at], k_buf[...], (((0,), (0,)), ((), ())),
                                          preferred_element_type=F32)
            for i in range(G):
                lt = s0 % L + i
                p = (lt - lo + L) % L
                if G == 1:
                    if j < NG - 1:
                        y_copy(k, lt, p).start()
                else:
                    @pl.when(p > 0)
                    def _():
                        y_copy(k, lt, p).start()
            if j == 0:
                @pl.when(k > 0)
                def _():
                    y_add(k - 1)
                    z_copy(k - 1).start()
        return carry

    lax.fori_loop(0, H, step, 0)
    y_add(H - 1)
    for k in range(H - 1):
        z_copy(k).wait_recv()
    for cp in in_copies:
        cp.wait()
    value = part[part_rows(shard), :]
    for k in range(H - 1):
        value = value + z_buf[k]
    grad = (acc_v[...] + value) / total[0:1, 0:1]
    g_buf[:, :acc_v.shape[1]] = grad
    g2 = grad * grad
    squares = g2 + EPS
    mean = jnp.sum(squares, axis=1, keepdims=True) / squares.shape[1]
    new_row = DECAY * row_v[...] + (1.0 - DECAY) * mean
    g_buf[:, acc_v.shape[1]:] = new_row

    g_cp = pltpu.make_async_copy(g_buf, g_out.at[rows], g_local.at[0])
    g_sib = rcopy(g_buf, g_out.at[rows], gc_send.at[0], gc_recv.at[0], dev_rep(sib))
    g_far = [rcopy(g_buf, g_out.at[rows], gx_send.at[q - 1], gx_recv.at[q - 1],
                   dev_rep(((x + q) % X) * 2 + c)) for q in range(1, X)]
    for cp in g_far:
        cp.start()
    g_sib.start()
    g_cp.start()

    col = jnp.sum(squares, axis=0, keepdims=True)
    upd = jnp.sum(g2 * (1.0 / new_row[:, :1]), axis=0, keepdims=True)
    w = w_v[...]
    wsq = jnp.sum(w * w, axis=0, keepdims=True)
    stats = jnp.concatenate([col, upd, wsq, jnp.zeros((5, col.shape[1]), F32)], axis=0)
    s_out[...] = reduce_all(stats, s1, s2, s3, b_send, b_recv)

    def g_fwd(q):
        src = ((x + X - q) % X) * 2 + c
        at = pl.ds(pl.multiple_of(src * sub, sub), sub)
        return rcopy(g_out.at[at], g_out.at[at], gf_send.at[q - 1], gf_recv.at[q - 1], dev_rep(sib))

    for q in range(1, X):
        g_far[q - 1].wait_recv()
        g_fwd(q).start()
    g_cp.wait()
    g_sib.wait()

    k_sib.wait_send()
    for q in range(1, X):
        k_far[q - 1].wait_send()
        k_fwd(q).wait_send()
        g_far[q - 1].wait_send()
        g_fwd(q).wait()

    def t_done(t, carry):
        for p in range(1, R):
            t_rem(t, p).wait_send()
        return carry

    lax.fori_loop(0, NCH, t_done, 0)
    for k in range(H):
        for p in range(1, L):
            y_copy(k, (lo + p) % L, p).wait_send()
        if k < H - 1:
            z_copy(k).wait_send()


def body(R, S, L, tokens_in, key_cotangent, token_counts, grad_accum, key_weight, row_moment, col_moment):
    tok, D = tokens_in.shape
    KV = key_cotangent.shape[1]
    H = S // L
    sub = D // (R * S)
    B = R * sub
    X = R // 2
    natural = sub % 128 == 0
    G = 1 if natural else 128 // sub
    NCH = S // G
    rows = jnp.broadcast_to(row_moment[:, None], (B, 128))
    tokens = tokens_in
    if not natural:
        tokens = tokens.reshape(tok, S, R, sub).transpose(0, 2, 1, 3).reshape(tok, D)
    dims = (R, S, H, L, G, sub, tok, natural)
    any_spec = pl.BlockSpec(memory_space=pl.ANY)
    vmem = pl.BlockSpec(memory_space=pltpu.VMEM)
    dma = pltpu.SemaphoreType.DMA
    n_all = (R - 1) + (L - 1) + (H - 1)
    X1 = max(X - 1, 1)
    grads, stats = pl.pallas_call(
        functools.partial(kernel, dims),
        out_shape=(jax.ShapeDtypeStruct((B, KV + 128), F32), jax.ShapeDtypeStruct((8, KV), F32)),
        in_specs=[any_spec, any_spec, pl.BlockSpec(memory_space=pltpu.SMEM), any_spec, any_spec, any_spec],
        out_specs=(any_spec, vmem),
        scratch_shapes=[
            pltpu.VMEM((R * tok, S * sub), jnp.bfloat16),
            pltpu.VMEM((R * tok, KV), jnp.bfloat16),
            pltpu.VMEM((S * sub, KV), F32),
            pltpu.VMEM((L - 1, H, sub, KV), F32),
            pltpu.VMEM((H - 1, sub, KV), F32),
            pltpu.VMEM((sub, KV), F32),
            pltpu.VMEM((sub, KV), F32),
            pltpu.VMEM((sub, 128), F32),
            pltpu.VMEM((sub, KV + 128), F32),
            pltpu.VMEM((R, 8, 128), F32),
            pltpu.VMEM((L, 8, 128), F32),
            pltpu.VMEM((H, 8, 128), F32),
            pltpu.VMEM((R, 8, KV), F32),
            pltpu.VMEM((L, 8, KV), F32),
            pltpu.VMEM((H, 8, KV), F32),
            dma((NCH,)), dma((R - 1, NCH)), dma((R - 1, NCH)),
            dma((1,)), dma((X1,)), dma((X1,)), dma((1,)), dma((1,)), dma((X1,)), dma((X1,)),
            dma((L - 1, H)), dma((L - 1, H)), dma((H - 1,)), dma((H - 1,)),
            dma((3,)),
            dma((1,)), dma((X1,)), dma((X1,)), dma((1,)), dma((1,)), dma((X1,)), dma((X1,)),
            dma((n_all,)), dma((n_all,)), dma((n_all,)), dma((n_all,)),
        ],
        compiler_params=pltpu.CompilerParams(collective_id=0, has_side_effects=True,
                                             vmem_limit_bytes=50 * 1024 * 1024),
        cost_estimate=pl.CostEstimate(flops=2 * tok * D * KV, bytes_accessed=24 * 1024 * 1024, transcendentals=0),
    )(tokens, key_cotangent, token_counts, grad_accum, key_weight, rows)
    entries = D * KV
    new_col = DECAY * col_moment + (1.0 - DECAY) * (stats[0] / D)
    update_sq = jnp.sum(stats[1] / new_col)
    weight_sum = jnp.sum(stats[2])
    new_row = grads[:, KV]
    clip = jnp.maximum(1.0, jnp.sqrt(update_sq / entries) / CLIP)
    direction = grads[:, :KV] * lax.rsqrt(new_row[:, None] * new_col[None, :]) / clip
    weight_rms = jnp.sqrt(weight_sum / entries)
    new_weight = key_weight - RATE * weight_rms * direction
    return (new_weight, direction, new_row, new_col)


def solution(mesh):
    R, S = mesh.shape["rep"], mesh.shape["shard"]
    in_specs = (
        P(("rep", "shard"), None),
        P(("rep", "shard"), None),
        P(None, ("rep", "shard")),
        P("shard", None),
        P("shard", None),
        P("shard"),
        P(),
    )
    out_specs = (P("shard", None), P("shard", None), P("shard"), P())
    return jax.shard_map(functools.partial(body, R, S, lo_size(S)), mesh=mesh, in_specs=in_specs,
                         out_specs=out_specs, check_vma=False)
```

```python
import functools

import jax
import jax.numpy as jnp
from jax import lax
from jax.experimental import pallas as pl
from jax.experimental.pallas import tpu as pltpu
from jax.sharding import PartitionSpec as P

EPS = 1e-30
DECAY = 0.6
CLIP = 1.0
RATE = 0.05
MESH = pl.DeviceIdType.MESH
EARLY = 0
WINDOW = 4
PIECES = 2
EAGER = 1
F32 = jnp.float32


def lo_size(shard):
    return 2 if shard == 8 else 4


def kernel(dims, t_ref, k_ref, cnt_ref, acc_ref, w_ref, row_ref, g_out, s_out,
           t_buf, k_buf, part, y_buf, z_buf, acc_v, w_v, row_v, g_buf,
           c1, c2, c3, s1, s2, s3,
           t_local, t_send, t_recv, k_local, kx_send, kx_recv, kc_send, kc_recv,
           kf_send, kf_recv, y_send, y_recv, z_send, z_recv, in_sem,
           g_local, gx_send, gx_recv, gc_send, gc_recv, gf_send, gf_recv,
           a_send, a_recv, b_send, b_recv):
    R, S, H, L, G, sub, tok, natural = dims
    X = R // 2
    NG = L // G
    NCH = H * NG
    width = G * sub
    D = S * R * sub
    rep, shard = lax.axis_index("rep"), lax.axis_index("shard")
    x, c = rep // 2, rep % 2
    sib = x * 2 + (1 - c)
    hi, lo = shard // L, shard % L
    g0 = lo // G

    def target(k):
        return (hi + jnp.where(k == H - 1, 0, (k + H // 2 - 1) % (H - 1) + 1)) % H

    def dev_rep(r):
        return (r, shard)

    def dev_lo(l):
        return (rep, hi * L + l)

    def dev_hi(h):
        return (rep, h * L + lo)

    def rcopy(src, dst, ss, rs, dev):
        return pltpu.make_async_remote_copy(src_ref=src, dst_ref=dst, send_sem=ss, recv_sem=rs,
                                            device_id=dev, device_id_type=MESH)

    barrier = pltpu.get_barrier_semaphore()
    peers = ([dev_rep((rep + p) % R) for p in range(1, R)] + [dev_lo((lo + p) % L) for p in range(1, L)]
             + [dev_hi((hi + p) % H) for p in range(1, H)])
    for dev in peers:
        pl.semaphore_signal(barrier, inc=1, device_id=dev, device_id_type=MESH)
    in_copies = []
    rows = pl.ds(pl.multiple_of(rep * sub, sub), sub)
    for i, (src, dst) in enumerate(((acc_ref, acc_v), (w_ref, w_v), (row_ref, row_v))):
        cp = pltpu.make_async_copy(src.at[rows], dst, in_sem.at[i])
        cp.start()
        in_copies.append(cp)
    my_tok = pl.ds(pl.multiple_of(rep * tok, tok), tok)
    k_cp = pltpu.make_async_copy(k_ref, k_buf.at[my_tok], k_local.at[0])
    k_cp.start()
    micro = cnt_ref.shape[0]
    count = cnt_ref[0, 0]
    for i in range(1, micro):
        count = count + cnt_ref[i, 0]
    k_cp.wait()
    keep = lax.broadcasted_iota(jnp.int32, (tok, 1), 0) < cnt_ref[micro - 1, 0]
    k_buf[my_tok, :] = jnp.where(keep, k_buf[my_tok, :], jnp.zeros((), k_buf.dtype))
    pl.semaphore_wait(barrier, len(peers))

    def reduce_all(first, b1, b2, b3, sends, recvs):
        value = first
        base = 0
        for buf, n, me, dev in ((b1, R, rep, dev_rep), (b2, L, lo, dev_lo), (b3, H, hi, dev_hi)):
            buf[me] = value
            cps = []
            for p in range(1, n):
                cp = rcopy(buf.at[me], buf.at[me], sends.at[base + p - 1], recvs.at[base + p - 1], dev((me + p) % n))
                cp.start()
                cps.append(cp)
            for cp in cps:
                cp.wait_send()
                cp.wait_recv()
            base += n - 1
            value = buf[0]
            for i in range(1, n):
                value = value + buf[i]
        return value

    k_sib = rcopy(k_buf.at[my_tok], k_buf.at[my_tok], kc_send.at[0], kc_recv.at[0], dev_rep(sib))
    k_far = [rcopy(k_buf.at[my_tok], k_buf.at[my_tok], kx_send.at[q - 1], kx_recv.at[q - 1],
                   dev_rep(((x + q) % X) * 2 + c)) for q in range(1, X)]
    for cp in k_far:
        cp.start()
    k_sib.start()

    def k_fwd(q):
        src = ((x + X - q) % X) * 2 + c
        at = pl.ds(pl.multiple_of(src * tok, tok), tok)
        return rcopy(k_buf.at[at], k_buf.at[at], kf_send.at[q - 1], kf_recv.at[q - 1], dev_rep(sib))

    def block_of(t):
        return target(t // NG) * L + ((g0 + 1 + t % NG) % NG) * G

    def t_cols(r, s0):
        if natural:
            off = s0 * (R * sub) + r * sub
        else:
            off = r * (S * sub) + s0 * sub
        return pl.ds(pl.multiple_of(off, width), width)

    def t_dst(s0):
        return t_buf.at[my_tok, pl.ds(pl.multiple_of(s0 * sub, width), width)]

    def t_loc(t):
        s0 = block_of(t)
        return pltpu.make_async_copy(t_ref.at[:, t_cols(rep, s0)], t_dst(s0), t_local.at[t])

    def t_rem(t, p):
        s0 = block_of(t)
        to = (rep + p) % R
        return rcopy(t_ref.at[:, t_cols(to, s0)], t_dst(s0), t_send.at[p - 1, t], t_recv.at[p - 1, t], dev_rep(to))

    def t_start(t):
        for p in range(1, R):
            t_rem(t, p).start()
        t_loc(t).start()

    for t in range(EARLY):
        t_start(t)

    total = reduce_all(jnp.full((8, 128), count.astype(F32)), c1, c2, c3, a_send, a_recv)

    for q in range(1, X):
        k_far[q - 1].wait_recv()
        k_fwd(q).start()
    for t in range(EARLY, min(WINDOW, NCH)):
        t_start(t)
    k_sib.wait_recv()
    for q in range(1, X):
        k_fwd(q).wait_recv()

    def part_rows(s, n=1):
        return pl.ds(pl.multiple_of(s * sub, n * sub), n * sub)

    piece = sub // PIECES

    def piece_rows(s, e):
        return pl.ds(pl.multiple_of(s * sub + e * piece, piece), piece)

    def at_piece(e):
        return pl.ds(e * piece, piece)

    def y_copy(k, lt, p, e):
        s = target(k) * L + lt
        return rcopy(part.at[piece_rows(s, e)], y_buf.at[p - 1, k, at_piece(e)], y_send.at[p - 1, k, e],
                     y_recv.at[p - 1, k, e], dev_lo(lt))

    def y_start(k, lt, p):
        for e in range(PIECES):
            y_copy(k, lt, p, e).start()

    def z_copy(k, e):
        h = target(k)
        return rcopy(part.at[piece_rows(h * L + lo, e)], z_buf.at[k, at_piece(e)], z_send.at[k, e],
                     z_recv.at[k, e], dev_hi(h))

    def y_add(k, e):
        at = piece_rows(target(k) * L + lo, e)
        for p in range(1, L):
            y_copy(k, (lo + p) % L, p, e).wait_recv()
        value = part[at, :]
        for p in range(1, L):
            value = value + y_buf[p - 1, k, e * piece:(e + 1) * piece, :]
        part[at, :] = value

    def step(k, carry):
        for j in range(NG):
            t = k * NG + j
            t_loc(t).wait()
            for p in range(1, R):
                t_rem(t, p).wait_recv()

            @pl.when(t + WINDOW < NCH)
            def _():
                t_start(t + WINDOW)

            s0 = block_of(t)
            at = pl.ds(pl.multiple_of(s0 * sub, width), width)
            part[at, :] = lax.dot_general(t_buf[:, at], k_buf[...], (((0,), (0,)), ((), ())),
                                          preferred_element_type=F32)
            for i in range(G):
                lt = s0 % L + i
                p = (lt - lo + L) % L
                if G == 1:
                    if j < NG - 1:
                        y_start(k, lt, p)
                else:
                    @pl.when(p > 0)
                    def _():
                        y_start(k, lt, p)
            if j == 0:
                @pl.when(k > 0)
                def _():
                    for e in range(EAGER, PIECES):
                        y_add(k - 1, e)
                        z_copy(k - 1, e).start()

        @pl.when(k < H - 1)
        def _():
            for e in range(EAGER):
                y_add(k, e)
                z_copy(k, e).start()
        return carry

    lax.fori_loop(0, H, step, 0)
    for e in range(PIECES):
        y_add(H - 1, e)
        for k in range(H - 1):
            z_copy(k, e).wait_recv()
    for cp in in_copies:
        cp.wait()
    value = part[part_rows(shard), :]
    for k in range(H - 1):
        value = value + z_buf[k]
    grad = (acc_v[...] + value) / total[0:1, 0:1]
    g_buf[:, :acc_v.shape[1]] = grad
    g2 = grad * grad
    squares = g2 + EPS
    mean = jnp.sum(squares, axis=1, keepdims=True) / squares.shape[1]
    new_row = DECAY * row_v[...] + (1.0 - DECAY) * mean
    g_buf[:, acc_v.shape[1]:] = new_row

    g_cp = pltpu.make_async_copy(g_buf, g_out.at[rows], g_local.at[0])
    g_sib = rcopy(g_buf, g_out.at[rows], gc_send.at[0], gc_recv.at[0], dev_rep(sib))
    g_far = [rcopy(g_buf, g_out.at[rows], gx_send.at[q - 1], gx_recv.at[q - 1],
                   dev_rep(((x + q) % X) * 2 + c)) for q in range(1, X)]
    for cp in g_far:
        cp.start()
    g_sib.start()
    g_cp.start()

    col = jnp.sum(squares, axis=0, keepdims=True)
    upd = jnp.sum(g2 * (1.0 / new_row[:, :1]), axis=0, keepdims=True)
    w = w_v[...]
    wsq = jnp.sum(w * w, axis=0, keepdims=True)
    stats = jnp.concatenate([col, upd, wsq, jnp.zeros((5, col.shape[1]), F32)], axis=0)
    s_out[...] = reduce_all(stats, s1, s2, s3, b_send, b_recv)

    def g_fwd(q):
        src = ((x + X - q) % X) * 2 + c
        at = pl.ds(pl.multiple_of(src * sub, sub), sub)
        return rcopy(g_out.at[at], g_out.at[at], gf_send.at[q - 1], gf_recv.at[q - 1], dev_rep(sib))

    for q in range(1, X):
        g_far[q - 1].wait_recv()
        g_fwd(q).start()
    g_cp.wait()
    g_sib.wait()

    k_sib.wait_send()
    for q in range(1, X):
        k_far[q - 1].wait_send()
        k_fwd(q).wait_send()
        g_far[q - 1].wait_send()
        g_fwd(q).wait()

    def t_done(t, carry):
        for p in range(1, R):
            t_rem(t, p).wait_send()
        return carry

    lax.fori_loop(0, NCH, t_done, 0)
    for k in range(H):
        for p in range(1, L):
            for e in range(PIECES):
                y_copy(k, (lo + p) % L, p, e).wait_send()
        if k < H - 1:
            for e in range(PIECES):
                z_copy(k, e).wait_send()


def body(R, S, L, tokens_in, key_cotangent, token_counts, grad_accum, key_weight, row_moment, col_moment):
    tok, D = tokens_in.shape
    KV = key_cotangent.shape[1]
    H = S // L
    sub = D // (R * S)
    B = R * sub
    X = R // 2
    natural = sub % 128 == 0
    G = 1 if natural else 128 // sub
    NCH = S // G
    rows = jnp.broadcast_to(row_moment[:, None], (B, 128))
    tokens = tokens_in
    if not natural:
        tokens = tokens.reshape(tok, S, R, sub).transpose(0, 2, 1, 3).reshape(tok, D)
    dims = (R, S, H, L, G, sub, tok, natural)
    any_spec = pl.BlockSpec(memory_space=pl.ANY)
    vmem = pl.BlockSpec(memory_space=pltpu.VMEM)
    dma = pltpu.SemaphoreType.DMA
    n_all = (R - 1) + (L - 1) + (H - 1)
    X1 = max(X - 1, 1)
    grads, stats = pl.pallas_call(
        functools.partial(kernel, dims),
        out_shape=(jax.ShapeDtypeStruct((B, KV + 128), F32), jax.ShapeDtypeStruct((8, KV), F32)),
        in_specs=[any_spec, any_spec, pl.BlockSpec(memory_space=pltpu.SMEM), any_spec, any_spec, any_spec],
        out_specs=(any_spec, vmem),
        scratch_shapes=[
            pltpu.VMEM((R * tok, S * sub), jnp.bfloat16),
            pltpu.VMEM((R * tok, KV), jnp.bfloat16),
            pltpu.VMEM((S * sub, KV), F32),
            pltpu.VMEM((L - 1, H, sub, KV), F32),
            pltpu.VMEM((H - 1, sub, KV), F32),
            pltpu.VMEM((sub, KV), F32),
            pltpu.VMEM((sub, KV), F32),
            pltpu.VMEM((sub, 128), F32),
            pltpu.VMEM((sub, KV + 128), F32),
            pltpu.VMEM((R, 8, 128), F32),
            pltpu.VMEM((L, 8, 128), F32),
            pltpu.VMEM((H, 8, 128), F32),
            pltpu.VMEM((R, 8, KV), F32),
            pltpu.VMEM((L, 8, KV), F32),
            pltpu.VMEM((H, 8, KV), F32),
            dma((NCH,)), dma((R - 1, NCH)), dma((R - 1, NCH)),
            dma((1,)), dma((X1,)), dma((X1,)), dma((1,)), dma((1,)), dma((X1,)), dma((X1,)),
            dma((L - 1, H, PIECES)), dma((L - 1, H, PIECES)), dma((H - 1, PIECES)), dma((H - 1, PIECES)),
            dma((3,)),
            dma((1,)), dma((X1,)), dma((X1,)), dma((1,)), dma((1,)), dma((X1,)), dma((X1,)),
            dma((n_all,)), dma((n_all,)), dma((n_all,)), dma((n_all,)),
        ],
        compiler_params=pltpu.CompilerParams(collective_id=0, has_side_effects=True,
                                             vmem_limit_bytes=50 * 1024 * 1024),
        cost_estimate=pl.CostEstimate(flops=2 * tok * D * KV, bytes_accessed=24 * 1024 * 1024, transcendentals=0),
    )(tokens, key_cotangent, token_counts, grad_accum, key_weight, rows)
    entries = D * KV
    new_col = DECAY * col_moment + (1.0 - DECAY) * (stats[0] / D)
    update_sq = jnp.sum(stats[1] / new_col)
    weight_sum = jnp.sum(stats[2])
    new_row = grads[:, KV]
    clip = jnp.maximum(1.0, jnp.sqrt(update_sq / entries) / CLIP)
    direction = grads[:, :KV] * lax.rsqrt(new_row[:, None] * new_col[None, :]) / clip
    weight_rms = jnp.sqrt(weight_sum / entries)
    new_weight = key_weight - RATE * weight_rms * direction
    return (new_weight, direction, new_row, new_col)


def solution(mesh):
    R, S = mesh.shape["rep"], mesh.shape["shard"]
    in_specs = (
        P(("rep", "shard"), None),
        P(("rep", "shard"), None),
        P(None, ("rep", "shard")),
        P("shard", None),
        P("shard", None),
        P("shard"),
        P(),
    )
    out_specs = (P("shard", None), P("shard", None), P("shard"), P())
    return jax.shard_map(functools.partial(body, R, S, lo_size(S)), mesh=mesh, in_specs=in_specs,
                         out_specs=out_specs, check_vma=False)
```

```python
import functools

import jax
import jax.numpy as jnp
from jax import lax
from jax.experimental import pallas as pl
from jax.experimental.pallas import tpu as pltpu
from jax.sharding import PartitionSpec as P

EPS = 1e-30
DECAY = 0.6
CLIP = 1.0
RATE = 0.05
MESH = pl.DeviceIdType.MESH
EARLY = 0
WINDOW = 4
PIECES = 4
EAGER = 2
F32 = jnp.float32


def lo_size(shard):
    return 2 if shard == 8 else 4


def kernel(dims, t_ref, k_ref, cnt_ref, acc_ref, w_ref, row_ref, g_out, s_out,
           t_buf, k_buf, part, y_buf, z_buf, acc_v, w_v, row_v, g_buf,
           c1, c2, c3, s1, s2, s3,
           t_local, t_send, t_recv, k_local, kx_send, kx_recv, kc_send, kc_recv,
           kf_send, kf_recv, y_send, y_recv, z_send, z_recv, in_sem,
           g_local, gx_send, gx_recv, gc_send, gc_recv, gf_send, gf_recv,
           a_send, a_recv, b_send, b_recv):
    R, S, H, L, G, sub, tok, natural = dims
    X = R // 2
    NG = L // G
    NCH = H * NG
    width = G * sub
    D = S * R * sub
    rep, shard = lax.axis_index("rep"), lax.axis_index("shard")
    x, c = rep // 2, rep % 2
    sib = x * 2 + (1 - c)
    hi, lo = shard // L, shard % L
    g0 = lo // G

    def target(k):
        return (hi + jnp.where(k == H - 1, 0, (k + H // 2 - 1) % (H - 1) + 1)) % H

    def dev_rep(r):
        return (r, shard)

    def dev_lo(l):
        return (rep, hi * L + l)

    def dev_hi(h):
        return (rep, h * L + lo)

    def rcopy(src, dst, ss, rs, dev):
        return pltpu.make_async_remote_copy(src_ref=src, dst_ref=dst, send_sem=ss, recv_sem=rs,
                                            device_id=dev, device_id_type=MESH)

    barrier = pltpu.get_barrier_semaphore()
    peers = ([dev_rep((rep + p) % R) for p in range(1, R)] + [dev_lo((lo + p) % L) for p in range(1, L)]
             + [dev_hi((hi + p) % H) for p in range(1, H)])
    for dev in peers:
        pl.semaphore_signal(barrier, inc=1, device_id=dev, device_id_type=MESH)
    in_copies = []
    rows = pl.ds(pl.multiple_of(rep * sub, sub), sub)
    for i, (src, dst) in enumerate(((acc_ref, acc_v), (w_ref, w_v), (row_ref, row_v))):
        cp = pltpu.make_async_copy(src.at[rows], dst, in_sem.at[i])
        cp.start()
        in_copies.append(cp)
    my_tok = pl.ds(pl.multiple_of(rep * tok, tok), tok)
    k_cp = pltpu.make_async_copy(k_ref, k_buf.at[my_tok], k_local.at[0])
    k_cp.start()
    micro = cnt_ref.shape[0]
    count = cnt_ref[0, 0]
    for i in range(1, micro):
        count = count + cnt_ref[i, 0]
    k_cp.wait()
    keep = lax.broadcasted_iota(jnp.int32, (tok, 1), 0) < cnt_ref[micro - 1, 0]
    k_buf[my_tok, :] = jnp.where(keep, k_buf[my_tok, :], jnp.zeros((), k_buf.dtype))
    pl.semaphore_wait(barrier, len(peers))

    def reduce_all(first, b1, b2, b3, sends, recvs):
        value = first
        base = 0
        for buf, n, me, dev in ((b1, R, rep, dev_rep), (b2, L, lo, dev_lo), (b3, H, hi, dev_hi)):
            buf[me] = value
            cps = []
            for p in range(1, n):
                cp = rcopy(buf.at[me], buf.at[me], sends.at[base + p - 1], recvs.at[base + p - 1], dev((me + p) % n))
                cp.start()
                cps.append(cp)
            for cp in cps:
                cp.wait_send()
                cp.wait_recv()
            base += n - 1
            value = buf[0]
            for i in range(1, n):
                value = value + buf[i]
        return value

    k_sib = rcopy(k_buf.at[my_tok], k_buf.at[my_tok], kc_send.at[0], kc_recv.at[0], dev_rep(sib))
    k_far = [rcopy(k_buf.at[my_tok], k_buf.at[my_tok], kx_send.at[q - 1], kx_recv.at[q - 1],
                   dev_rep(((x + q) % X) * 2 + c)) for q in range(1, X)]
    for cp in k_far:
        cp.start()
    k_sib.start()

    def k_fwd(q):
        src = ((x + X - q) % X) * 2 + c
        at = pl.ds(pl.multiple_of(src * tok, tok), tok)
        return rcopy(k_buf.at[at], k_buf.at[at], kf_send.at[q - 1], kf_recv.at[q - 1], dev_rep(sib))

    def block_of(t):
        return target(t // NG) * L + ((g0 + 1 + t % NG) % NG) * G

    def t_cols(r, s0):
        if natural:
            off = s0 * (R * sub) + r * sub
        else:
            off = r * (S * sub) + s0 * sub
        return pl.ds(pl.multiple_of(off, width), width)

    def t_dst(s0):
        return t_buf.at[my_tok, pl.ds(pl.multiple_of(s0 * sub, width), width)]

    def t_loc(t):
        s0 = block_of(t)
        return pltpu.make_async_copy(t_ref.at[:, t_cols(rep, s0)], t_dst(s0), t_local.at[t])

    def t_rem(t, p):
        s0 = block_of(t)
        to = (rep + p) % R
        return rcopy(t_ref.at[:, t_cols(to, s0)], t_dst(s0), t_send.at[p - 1, t], t_recv.at[p - 1, t], dev_rep(to))

    def t_start(t):
        for p in range(1, R):
            t_rem(t, p).start()
        t_loc(t).start()

    for t in range(EARLY):
        t_start(t)

    total = reduce_all(jnp.full((8, 128), count.astype(F32)), c1, c2, c3, a_send, a_recv)

    for q in range(1, X):
        k_far[q - 1].wait_recv()
        k_fwd(q).start()
    for t in range(EARLY, min(WINDOW, NCH)):
        t_start(t)
    k_sib.wait_recv()
    for q in range(1, X):
        k_fwd(q).wait_recv()

    def part_rows(s, n=1):
        return pl.ds(pl.multiple_of(s * sub, n * sub), n * sub)

    piece = sub // PIECES

    def piece_rows(s, e):
        return pl.ds(pl.multiple_of(s * sub + e * piece, piece), piece)

    def at_piece(e):
        return pl.ds(e * piece, piece)

    def y_copy(k, lt, p, e):
        s = target(k) * L + lt
        return rcopy(part.at[piece_rows(s, e)], y_buf.at[p - 1, k, at_piece(e)], y_send.at[p - 1, k, e],
                     y_recv.at[p - 1, k, e], dev_lo(lt))

    def y_start(k, lt, p):
        for e in range(PIECES):
            y_copy(k, lt, p, e).start()

    def z_copy(k, e):
        h = target(k)
        return rcopy(part.at[piece_rows(h * L + lo, e)], z_buf.at[k, at_piece(e)], z_send.at[k, e],
                     z_recv.at[k, e], dev_hi(h))

    def y_add(k, e):
        at = piece_rows(target(k) * L + lo, e)
        for p in range(1, L):
            y_copy(k, (lo + p) % L, p, e).wait_recv()
        value = part[at, :]
        for p in range(1, L):
            value = value + y_buf[p - 1, k, e * piece:(e + 1) * piece, :]
        part[at, :] = value

    def step(k, carry):
        for j in range(NG):
            t = k * NG + j
            t_loc(t).wait()
            for p in range(1, R):
                t_rem(t, p).wait_recv()

            @pl.when(t + WINDOW < NCH)
            def _():
                t_start(t + WINDOW)

            s0 = block_of(t)
            at = pl.ds(pl.multiple_of(s0 * sub, width), width)
            part[at, :] = lax.dot_general(t_buf[:, at], k_buf[...], (((0,), (0,)), ((), ())),
                                          preferred_element_type=F32)
            for i in range(G):
                lt = s0 % L + i
                p = (lt - lo + L) % L
                if G == 1:
                    if j < NG - 1:
                        y_start(k, lt, p)
                else:
                    @pl.when(p > 0)
                    def _():
                        y_start(k, lt, p)
            if j == 0:
                @pl.when(k > 0)
                def _():
                    for e in range(EAGER, PIECES):
                        y_add(k - 1, e)
                        z_copy(k - 1, e).start()

        @pl.when(k < H - 1)
        def _():
            for e in range(EAGER):
                y_add(k, e)
                z_copy(k, e).start()
        return carry

    lax.fori_loop(0, H, step, 0)
    for cp in in_copies:
        cp.wait()
    w = w_v[...]
    wsq = jnp.sum(w * w, axis=0, keepdims=True)
    kv = acc_v.shape[1]

    def out_rows(r, e):
        return g_out.at[pl.ds(pl.multiple_of(r * sub + e * piece, piece), piece)]

    def g_cp(e):
        return pltpu.make_async_copy(g_buf.at[at_piece(e)], out_rows(rep, e), g_local.at[e])

    def g_sib(e):
        return rcopy(g_buf.at[at_piece(e)], out_rows(rep, e), gc_send.at[e], gc_recv.at[e], dev_rep(sib))

    def g_far(q, e):
        return rcopy(g_buf.at[at_piece(e)], out_rows(rep, e), gx_send.at[q - 1, e], gx_recv.at[q - 1, e],
                     dev_rep(((x + q) % X) * 2 + c))

    def g_fwd(q, e):
        src = ((x + X - q) % X) * 2 + c
        return rcopy(out_rows(src, e), out_rows(src, e), gf_send.at[q - 1, e], gf_recv.at[q - 1, e], dev_rep(sib))

    col = jnp.zeros((1, kv), F32)
    upd = jnp.zeros((1, kv), F32)
    for e in range(PIECES):
        y_add(H - 1, e)
        at = slice(e * piece, (e + 1) * piece)
        value = part[piece_rows(shard, e), :]
        for k in range(H - 1):
            z_copy(k, e).wait_recv()
            value = value + z_buf[k, at, :]
        grad = (acc_v[at, :] + value) / total[0:1, 0:1]
        g_buf[at, :kv] = grad
        g2 = grad * grad
        squares = g2 + EPS
        mean = jnp.sum(squares, axis=1, keepdims=True) / kv
        new_row = DECAY * row_v[at, :] + (1.0 - DECAY) * mean
        g_buf[at, kv:] = new_row
        for q in range(1, X):
            g_far(q, e).start()
        g_sib(e).start()
        g_cp(e).start()
        col = col + jnp.sum(squares, axis=0, keepdims=True)
        upd = upd + jnp.sum(g2 * (1.0 / new_row[:, :1]), axis=0, keepdims=True)

    stats = jnp.concatenate([col, upd, wsq, jnp.zeros((5, kv), F32)], axis=0)
    s_out[...] = reduce_all(stats, s1, s2, s3, b_send, b_recv)

    for e in range(PIECES):
        for q in range(1, X):
            g_far(q, e).wait_recv()
            g_fwd(q, e).start()
    for e in range(PIECES):
        g_cp(e).wait()
        g_sib(e).wait()

    k_sib.wait_send()
    for q in range(1, X):
        k_far[q - 1].wait_send()
        k_fwd(q).wait_send()
        for e in range(PIECES):
            g_far(q, e).wait_send()
            g_fwd(q, e).wait()

    def t_done(t, carry):
        for p in range(1, R):
            t_rem(t, p).wait_send()
        return carry

    lax.fori_loop(0, NCH, t_done, 0)
    for k in range(H):
        for p in range(1, L):
            for e in range(PIECES):
                y_copy(k, (lo + p) % L, p, e).wait_send()
        if k < H - 1:
            for e in range(PIECES):
                z_copy(k, e).wait_send()


def body(R, S, L, tokens_in, key_cotangent, token_counts, grad_accum, key_weight, row_moment, col_moment):
    tok, D = tokens_in.shape
    KV = key_cotangent.shape[1]
    H = S // L
    sub = D // (R * S)
    B = R * sub
    X = R // 2
    natural = sub % 128 == 0
    G = 1 if natural else 128 // sub
    NCH = S // G
    rows = jnp.broadcast_to(row_moment[:, None], (B, 128))
    tokens = tokens_in
    if not natural:
        tokens = tokens.reshape(tok, S, R, sub).transpose(0, 2, 1, 3).reshape(tok, D)
    dims = (R, S, H, L, G, sub, tok, natural)
    any_spec = pl.BlockSpec(memory_space=pl.ANY)
    vmem = pl.BlockSpec(memory_space=pltpu.VMEM)
    dma = pltpu.SemaphoreType.DMA
    n_all = (R - 1) + (L - 1) + (H - 1)
    X1 = max(X - 1, 1)
    grads, stats = pl.pallas_call(
        functools.partial(kernel, dims),
        out_shape=(jax.ShapeDtypeStruct((B, KV + 128), F32), jax.ShapeDtypeStruct((8, KV), F32)),
        in_specs=[any_spec, any_spec, pl.BlockSpec(memory_space=pltpu.SMEM), any_spec, any_spec, any_spec],
        out_specs=(any_spec, vmem),
        scratch_shapes=[
            pltpu.VMEM((R * tok, S * sub), jnp.bfloat16),
            pltpu.VMEM((R * tok, KV), jnp.bfloat16),
            pltpu.VMEM((S * sub, KV), F32),
            pltpu.VMEM((L - 1, H, sub, KV), F32),
            pltpu.VMEM((H - 1, sub, KV), F32),
            pltpu.VMEM((sub, KV), F32),
            pltpu.VMEM((sub, KV), F32),
            pltpu.VMEM((sub, 128), F32),
            pltpu.VMEM((sub, KV + 128), F32),
            pltpu.VMEM((R, 8, 128), F32),
            pltpu.VMEM((L, 8, 128), F32),
            pltpu.VMEM((H, 8, 128), F32),
            pltpu.VMEM((R, 8, KV), F32),
            pltpu.VMEM((L, 8, KV), F32),
            pltpu.VMEM((H, 8, KV), F32),
            dma((NCH,)), dma((R - 1, NCH)), dma((R - 1, NCH)),
            dma((1,)), dma((X1,)), dma((X1,)), dma((1,)), dma((1,)), dma((X1,)), dma((X1,)),
            dma((L - 1, H, PIECES)), dma((L - 1, H, PIECES)), dma((H - 1, PIECES)), dma((H - 1, PIECES)),
            dma((3,)),
            dma((PIECES,)), dma((X1, PIECES)), dma((X1, PIECES)), dma((PIECES,)), dma((PIECES,)),
            dma((X1, PIECES)), dma((X1, PIECES)),
            dma((n_all,)), dma((n_all,)), dma((n_all,)), dma((n_all,)),
        ],
        compiler_params=pltpu.CompilerParams(collective_id=0, has_side_effects=True,
                                             vmem_limit_bytes=50 * 1024 * 1024),
        cost_estimate=pl.CostEstimate(flops=2 * tok * D * KV, bytes_accessed=24 * 1024 * 1024, transcendentals=0),
    )(tokens, key_cotangent, token_counts, grad_accum, key_weight, rows)
    entries = D * KV
    new_col = DECAY * col_moment + (1.0 - DECAY) * (stats[0] / D)
    update_sq = jnp.sum(stats[1] / new_col)
    weight_sum = jnp.sum(stats[2])
    new_row = grads[:, KV]
    clip = jnp.maximum(1.0, jnp.sqrt(update_sq / entries) / CLIP)
    direction = grads[:, :KV] * lax.rsqrt(new_row[:, None] * new_col[None, :]) / clip
    weight_rms = jnp.sqrt(weight_sum / entries)
    new_weight = key_weight - RATE * weight_rms * direction
    return (new_weight, direction, new_row, new_col)


def solution(mesh):
    R, S = mesh.shape["rep"], mesh.shape["shard"]
    in_specs = (
        P(("rep", "shard"), None),
        P(("rep", "shard"), None),
        P(None, ("rep", "shard")),
        P("shard", None),
        P("shard", None),
        P("shard"),
        P(),
    )
    out_specs = (P("shard", None), P("shard", None), P("shard"), P())
    return jax.shard_map(functools.partial(body, R, S, lo_size(S)), mesh=mesh, in_specs=in_specs,
                         out_specs=out_specs, check_vma=False)
```
